32 devices in a mesh: dp: 8 (over y, x, core), mp: 4 (over z).
Axes of the slice: x: 2, y: 2, z: 4, core: 2. Of those that a mesh axis runs over, the one named last changes fastest.
Arguments:
- tokens: bfloat16 [2048, 4096], P('dp'), may hold values from -32 to 32
- weights: bfloat16 [4096, 2, 3, 4096], P('dp', None, None, 'mp'), may hold values from -1 to 1
- block_modality: int32 [16], replicated, may hold values from 0 to 1
- doc_ids: int32 [2048], replicated, may hold values from 0 to 15, never falling along the last dimension, each value on 1 to 1024 neighbouring positions
- grad_out: bfloat16 [2048, 4096], P('dp', 'mp'), may hold values from -6 to 6
Outputs:
- attended: bfloat16 [2048, 4096], P('dp', 'mp')
- grad_tokens: bfloat16 [2048, 4096], P('dp', 'mp')
- grad_weights: bfloat16 [4096, 2, 3, 4096], P('dp', None, None, 'mp')
The draws below stay inside these ranges and needn't reach their ends.
Inputs may be any that keep to these rules, and one draw needn't show every extreme that they name: doc_ids never falls along the sequence; a document is a run of equal ids of at most 1024 tokens, and one document has exactly 1024.
All inputs are finite; a program needn't handle non-finite values.
Results may differ from the reference program's by a relative error of at most 0.025.
Values may be sent and summed in bfloat16 or wider, within the bound.
A program may use at most 192 MiB of HBM per device.

```python
import math
import jax
import jax.numpy as jnp
import numpy as np
from jax import lax

D = 4096
HEADS = 32
HD = 128
BLOCK = 128
SPAN = 4
TOK_DEV = 256
TOKENS = 2048
HQ = 4096
DOCS = 16
MAXDOC = 1024
N_DP = 8
N_MP = 4


def draw_tokens(key, part):
    own_key = jax.random.fold_in(key, 11)
    base_key = jax.random.fold_in(own_key, 0)
    base = jax.random.normal(base_key, (TOKENS, D), jnp.float32)
    return jnp.clip(base, -6.0, 6.0).astype(jnp.bfloat16)


def draw_weights(key, part):
    own_key = jax.random.fold_in(key, 23)
    single_key = jax.random.fold_in(own_key, 1)
    single = jax.random.normal(single_key, (D, 2, 3, HQ), jnp.float32)
    return (jnp.clip(single, -6.0, 6.0) * D ** (-0.5)).astype(jnp.bfloat16)


def plant(values, stream_key, low, top_value):
    extent = values.shape
    spot = [jax.random.randint(jax.random.fold_in(stream_key, axis), (), 0, extent[axis]) for axis in range(len(extent))]
    values = values.at[tuple(spot)].set(low)
    longest = extent.index(max(extent))
    spot[longest] = (spot[longest] + 1) % extent[longest]
    return values.at[tuple(spot)].set(top_value)


def level_of(rng, extent, pieces, smallest, largest):
    gain, own = 1.0, jax.random.fold_in(rng, 6)
    for dim, blocks in pieces:
        steps = jnp.exp(jax.random.uniform(jax.random.fold_in(own, dim), (blocks,), jnp.float32, smallest / len(pieces), largest / len(pieces)))
        gain = gain * jnp.repeat(steps, extent[dim] // blocks).reshape([-1 if axis == dim else 1 for axis in range(len(extent))])
    return gain


def profile(count, total, most, skew):
    portions = [(1 << 20) // math.isqrt(grade ** skew) + 1 for grade in range(2, count + 1)]
    spare, holding = total - most - (count - 1), [1] * (count - 1)
    while spare > 0:
        free = [i for i in range(count - 1) if holding[i] < most]
        mass, remaining = sum([portions[i] for i in free]), spare
        for i in free:
            addition = min(most - holding[i], max(1, remaining * portions[i] // mass), spare)
            holding[i] = holding[i] + addition
            spare = spare - addition
    return np.array([most] + holding)


def ragged(stream_key, count, total, limit, slope):
    if count == 2:
        one = jax.random.randint(stream_key, (), max(1, total - limit), min(limit, total - 1) + 1)
        return jnp.stack([one, total - one])
    sizes = jnp.asarray(profile(count, total, limit, slope), jnp.int32)
    twos = (count - 1) // 2
    source_of, taker = sizes[1:1 + 2 * twos:2], sizes[2:2 + 2 * twos:2]
    slack = jnp.minimum(source_of - 1, limit - taker)
    shifted = jax.random.randint(jax.random.fold_in(stream_key, 1), (twos,), 0, 1 << 20) % (slack + 1)
    sizes = sizes.at[1:1 + 2 * twos:2].set(source_of - shifted).at[2:2 + 2 * twos:2].set(taker + shifted)
    return sizes[jax.random.permutation(jax.random.fold_in(stream_key, 2), count)]


def gaussian(key, shape, scale, limit, cuts=(), kind=jnp.bfloat16):
    values = scale * jax.random.normal(key, shape, jnp.float32)
    if cuts:
        values = values * level_of(key, shape, cuts, -0.22, 0.18)
    return jnp.clip(values, -limit, limit).astype(kind)


def setup_inputs(seed: int = 0) -> dict:
    splits = jax.random.split(jax.random.key(seed), 6)
    return {
        "tokens": draw_tokens(jax.random.fold_in(splits[5], 71), 0),
        "weights": draw_weights(jax.random.fold_in(splits[5], 71), 0),
        "block_modality": plant(jax.random.randint(splits[2], (TOKENS // BLOCK,), 0, 2), jax.random.fold_in(splits[2], 1), 0, 1).astype(jnp.int32),
        "doc_ids": jnp.searchsorted(jnp.cumsum(ragged(splits[3], DOCS, TOKENS, MAXDOC, 2)), jnp.arange(TOKENS), side="right").astype(jnp.int32),
        "grad_out": gaussian(splits[4], (TOKENS, HQ), 1.0, 6.0, ((0, 8), (1, 4))),
    }


def reference(tokens, weights, block_modality, doc_ids, grad_out):
    scale_factor = HD ** -0.5
    block_count = TOKENS // BLOCK
    flat_weights = weights.reshape(D, 2, 3 * HQ)

    def project(pair):
        block_rows, modality = pair
        chosen = lax.dynamic_index_in_dim(flat_weights, modality, 1, keepdims=False)
        return jnp.dot(block_rows, chosen, preferred_element_type=jnp.float32).astype(jnp.bfloat16)

    qkv = lax.map(project, (tokens.reshape(block_count, BLOCK, D), block_modality))
    qkv = qkv.reshape(TOKENS, 3, HEADS, HD)
    queries = qkv[:, 0]
    front_pad = SPAN * TOK_DEV
    window_len = (SPAN + 1) * TOK_DEV
    zero_pad = jnp.zeros((front_pad, HEADS, HD), jnp.bfloat16)
    keys_pad = jnp.concatenate([zero_pad, qkv[:, 1]], 0)
    values_pad = jnp.concatenate([zero_pad, qkv[:, 2]], 0)
    docs_pad = jnp.concatenate([jnp.full((front_pad,), -1, jnp.int32), doc_ids], 0)
    upstream = grad_out.reshape(TOKENS, HEADS, HD)

    def one_block(accum, index):
        first_row = index * TOK_DEV
        query_rows = lax.dynamic_slice_in_dim(queries, first_row, TOK_DEV, 0).astype(jnp.float32)
        key_rows = lax.dynamic_slice_in_dim(keys_pad, first_row, window_len, 0).astype(jnp.float32)
        value_rows = lax.dynamic_slice_in_dim(values_pad, first_row, window_len, 0).astype(jnp.float32)
        query_docs = lax.dynamic_slice_in_dim(doc_ids, first_row, TOK_DEV, 0)
        key_docs = lax.dynamic_slice_in_dim(docs_pad, first_row, window_len, 0)
        offsets = jnp.arange(window_len, dtype=jnp.int32) - front_pad
        allowed = (key_docs[None, :] == query_docs[:, None]) & (offsets[None, :] <= jnp.arange(TOK_DEV, dtype=jnp.int32)[:, None])
        scores = jnp.einsum("qhd,khd->hqk", query_rows, key_rows) * scale_factor
        scores = jnp.where(allowed[None], scores, -1e30)
        top_score = jnp.max(scores, axis=-1, keepdims=True)
        expos = jnp.where(allowed[None], jnp.exp(scores - top_score), 0.0)
        probs_f = expos / jnp.sum(expos, axis=-1, keepdims=True)
        probs = probs_f.astype(jnp.bfloat16).astype(jnp.float32)
        result = jnp.einsum("hqk,khd->qhd", probs, value_rows).astype(jnp.bfloat16)
        grad_rows = lax.dynamic_slice_in_dim(upstream, first_row, TOK_DEV, 0).astype(jnp.float32)
        dprob = jnp.einsum("qhd,khd->hqk", grad_rows, value_rows)
        row_delta = jnp.sum(probs_f * dprob, axis=-1, keepdims=True)
        dscore = (probs_f * (dprob - row_delta)).astype(jnp.bfloat16).astype(jnp.float32)
        grad_q = jnp.einsum("hqk,khd->qhd", dscore, key_rows) * scale_factor
        grad_k = jnp.einsum("hqk,qhd->khd", dscore, query_rows) * scale_factor
        grad_v = jnp.einsum("hqk,qhd->khd", probs, grad_rows)
        window = lax.dynamic_slice_in_dim(accum, first_row, window_len, 0) + jnp.stack([grad_k, grad_v], 1)
        accum = lax.dynamic_update_slice_in_dim(accum, window, first_row, 0)
        return accum, (result, grad_q)

    accum_init = jnp.zeros((front_pad + TOKENS, 2, HEADS, HD), jnp.float32)
    accum, (results, grad_qs) = lax.scan(one_block, accum_init, jnp.arange(N_DP, dtype=jnp.int32))
    attended = results.reshape(TOKENS, HQ)
    grad_q_all = grad_qs.reshape(TOKENS, 1, HEADS, HD)
    grad_kv = accum[front_pad:]
    dqkv = jnp.concatenate([grad_q_all, grad_kv], 1).astype(jnp.bfloat16).reshape(TOKENS, 3 * HQ)

    token_mods = jnp.broadcast_to(block_modality[:, None], (block_count, BLOCK)).reshape(TOKENS)
    grad_list = []
    for modality in range(2):
        chosen_rows = jnp.where(token_mods[:, None] == modality, tokens, jnp.zeros_like(tokens))
        grad_list.append(lax.dot_general(chosen_rows, dqkv, (((0,), (0,)), ((), ())), preferred_element_type=jnp.float32))
    grad_weights = jnp.stack(grad_list, 1).astype(jnp.bfloat16).reshape(D, 2, 3, HQ)

    group_weights = weights.reshape(D, 2, 3, N_MP, HQ // N_MP)
    group_grads = dqkv.reshape(block_count, BLOCK, 3, N_MP, HQ // N_MP)

    def input_block(pair):
        block_grads, modality = pair
        chosen = lax.dynamic_index_in_dim(group_weights, modality, 1, keepdims=False).astype(jnp.float32)
        parts = jnp.einsum("nkjh,dkjh->jnd", block_grads.astype(jnp.float32), chosen)
        parts = parts.astype(jnp.bfloat16).astype(jnp.float32)
        return jnp.sum(parts, axis=0).astype(jnp.bfloat16)

    grad_tokens = lax.map(input_block, (group_grads, block_modality)).reshape(TOKENS, D)
    return attended, grad_tokens, grad_weights
```

```python
import functools

import jax
import jax.numpy as jnp
from jax import lax
from jax.experimental import pallas as pl
from jax.experimental.pallas import tpu as pltpu
from jax.sharding import PartitionSpec as P

HD = 128
BLOCK = 128
SPAN = 4


def shifted(block, axis, distance):
    devices = range(lax.axis_size(axis))
    route = [(i - distance, i) for i in devices if i - distance in devices]
    return lax.ppermute(block, axis, route)


def select_product(block_rows, modality, text_mat, image_mat, contract):
    contraction = (((1,), (contract,)), ((), ()))
    return lax.cond(
        modality == 0,
        lambda: lax.dot_general(
            block_rows, text_mat, contraction, preferred_element_type=jnp.float32
        ),
        lambda: lax.dot_general(
            block_rows, image_mat, contraction, preferred_element_type=jnp.float32
        ),
    )


def blockwise(row_data, modalities, text_mat, image_mat, contract):
    blocks = row_data.reshape(modalities.shape[0], BLOCK, row_data.shape[1])

    def one_block(block_pair):
        return select_product(block_pair[0], block_pair[1], text_mat, image_mat, contract)

    result = lax.map(one_block, (blocks, modalities))
    return result.reshape(row_data.shape[0], result.shape[2])


def windowed(tokens, weights, block_modality, doc_ids, grad_out):
    local_rows = tokens.shape[0]
    width_rows = weights.shape[0]
    head_width = weights.shape[3]
    head_count = head_width // HD
    dp_devices = lax.axis_size("dp")
    local_blocks = local_rows // BLOCK
    front_pad = SPAN * local_rows
    window_len = front_pad + local_rows
    my_index = lax.axis_index("dp")
    scale_factor = HD ** (-0.5)
    my_mods = lax.dynamic_slice_in_dim(block_modality, my_index * local_blocks, local_blocks, 0)
    flat_weights = weights.reshape(width_rows, 2, 3 * head_width)
    text_local = flat_weights[:, 0]
    image_local = flat_weights[:, 1]
    columns = lax.all_to_all(tokens, "dp", split_axis=1, concat_axis=0, tiled=True)
    text_whole, image_whole = (
        lax.all_gather(text_local, "dp", axis=0, tiled=True),
        lax.all_gather(image_local, "dp", axis=0, tiled=True),
    )
    summed = blockwise(tokens, my_mods, text_whole, image_whole, 0)
    qkv = summed.astype(jnp.bfloat16).reshape(local_rows, 3, head_count, HD)
    queries = qkv[:, 0]
    key_values = qkv[:, 1:]
    received = []
    for distance in range(SPAN, 0, -1):
        received.append(shifted(key_values, "dp", distance))
    window = jnp.concatenate(received + [key_values], 0)
    key_rows = window[:, 0]
    value_rows = window[:, 1]
    docs_pad = jnp.concatenate([jnp.full((front_pad,), -1, jnp.int32), doc_ids], 0)
    key_docs = lax.dynamic_slice_in_dim(docs_pad, my_index * local_rows, window_len, 0)
    query_docs = lax.dynamic_slice_in_dim(doc_ids, my_index * local_rows, local_rows, 0)
    offsets = jnp.arange(window_len, dtype=jnp.int32) - front_pad
    allowed = (key_docs[None, :] == query_docs[:, None]) & (
        offsets[None, :] <= jnp.arange(local_rows, dtype=jnp.int32)[:, None]
    )
    scores = (
        jnp.einsum("qhd,khd->hqk", queries, key_rows, preferred_element_type=jnp.float32)
        * scale_factor
    )
    scores = jnp.where(allowed[None], scores, -1e30)
    top_score = jnp.max(scores, axis=-1, keepdims=True)
    expos = jnp.where(allowed[None], jnp.exp(scores - top_score), 0.0)
    probs_f = expos / jnp.sum(expos, axis=-1, keepdims=True)
    probs = probs_f.astype(jnp.bfloat16)
    attended = jnp.einsum("hqk,khd->qhd", probs, value_rows, preferred_element_type=jnp.float32)
    attended = attended.astype(jnp.bfloat16).reshape(local_rows, head_width)
    upstream = grad_out.reshape(local_rows, head_count, HD)
    dprob = jnp.einsum("qhd,khd->hqk", upstream, value_rows, preferred_element_type=jnp.float32)
    row_delta = jnp.sum(probs_f * dprob, axis=-1, keepdims=True)
    dscore = (probs_f * (dprob - row_delta)).astype(jnp.bfloat16)
    grad_q = (
        jnp.einsum("hqk,khd->qhd", dscore, key_rows, preferred_element_type=jnp.float32)
        * scale_factor
    )
    grad_k = (
        jnp.einsum("hqk,qhd->khd", dscore, queries, preferred_element_type=jnp.float32)
        * scale_factor
    )
    grad_v = jnp.einsum("hqk,qhd->khd", probs, upstream, preferred_element_type=jnp.float32)
    window_grads = jnp.stack([grad_k, grad_v], 1)
    own_grads = window_grads[front_pad:]
    for distance in range(1, SPAN + 1):
        lower_edge = front_pad - distance * local_rows
        sent_block = window_grads[lower_edge : lower_edge + local_rows]
        own_grads = own_grads + shifted(sent_block.astype(jnp.bfloat16), "dp", -distance).astype(
            sent_block.dtype
        )
    dqkv = (
        jnp.concatenate([grad_q[:, None], own_grads], 1)
        .astype(jnp.bfloat16)
        .reshape(local_rows, 3 * head_width)
    )
    gathered = lax.all_gather(dqkv, "dp", axis=0, tiled=True)
    column_groups = columns.reshape(dp_devices, local_blocks, BLOCK, width_rows)
    grad_groups = gathered.reshape(dp_devices, local_blocks, BLOCK, 3 * head_width)
    modality_groups = block_modality.reshape(dp_devices, local_blocks)
    modality_range = jnp.arange(2, dtype=jnp.int32)

    def accumulate(running, triple):
        column_group, grad_group, group_mods = triple
        per_block = jnp.einsum(
            "bnf,bnc->bfc", column_group, grad_group, preferred_element_type=jnp.float32
        )
        selector = (group_mods[:, None] == modality_range[None, :]).astype(jnp.float32)
        return (running + jnp.sum(selector[:, :, None, None] * per_block[:, None], axis=0), None)

    weight_sum, unused = lax.scan(
        accumulate,
        jnp.zeros((2, width_rows, 3 * head_width), jnp.float32),
        (column_groups, grad_groups, modality_groups),
    )
    grad_weights = (
        jnp.transpose(weight_sum, (1, 0, 2))
        .astype(jnp.bfloat16)
        .reshape(width_rows, 2, 3, head_width)
    )
    input_terms = blockwise(dqkv, my_mods, text_whole, image_whole, 1)
    grad_tokens = lax.psum_scatter(
        input_terms.astype(jnp.bfloat16), "mp", scatter_dimension=1, tiled=True
    )
    return (attended, grad_tokens, grad_weights)


VMEM_LIMIT = 56 * 1024 * 1024
NT = (((1,), (1,)), ((), ()))
TN = (((0,), (0,)), ((), ()))


def dot_f32(a, b, dims=(((1,), (0,)), ((), ()))):
    return lax.dot_general(a, b, dims, preferred_element_type=jnp.float32)


def params():
    return pltpu.CompilerParams(vmem_limit_bytes=VMEM_LIMIT)


def project_kernel(pair, mods_ref, x_ref, w_ref, out_ref):
    blocks = x_ref.shape[0] // BLOCK

    def one(b, carry):
        rows = pl.ds(pl.multiple_of(b * BLOCK, BLOCK), BLOCK)
        x = x_ref[rows, :]
        modality = mods_ref[b]
        for p in range(3):
            y = dot_f32(x, w_ref[modality, p]).astype(jnp.bfloat16)
            for h in range(pair):
                out_ref[h, rows, p * HD : (p + 1) * HD] = y[:, h * HD : (h + 1) * HD]
        return carry

    lax.fori_loop(0, blocks, one, 0, unroll=4)


def project(columns, planes, block_modality, pair):
    rows, width = columns.shape
    heads = planes.shape[3] // HD
    return pl.pallas_call(
        functools.partial(project_kernel, pair),
        out_shape=jax.ShapeDtypeStruct((heads, rows, 3 * HD), jnp.bfloat16),
        grid_spec=pltpu.PrefetchScalarGridSpec(
            num_scalar_prefetch=1,
            grid=(heads // pair,),
            in_specs=[
                pl.BlockSpec((rows, width), lambda h, m: (0, 0)),
                pl.BlockSpec((2, 3, width, pair * HD), lambda h, m: (0, 0, 0, h)),
            ],
            out_specs=pl.BlockSpec((pair, rows, 3 * HD), lambda h, m: (h, 0, 0)),
        ),
        compiler_params=params(),
        name="project",
    )(block_modality, columns, planes)


def attention_kernel(step, window, qkv_ref, g_ref, col_ref, row_ref, att_ref, grad_ref, dk_acc, dv_acc):
    i = pl.program_id(1)
    scale = HD ** (-0.5)
    low = pl.multiple_of(jnp.maximum((i + 1) * step - window, 0), step)
    mine = pl.ds(pl.multiple_of(i * step, step), step)
    seen = pl.ds(low, window)

    @pl.when(i == 0)
    def _():
        dk_acc[...] = jnp.zeros_like(dk_acc)
        dv_acc[...] = jnp.zeros_like(dv_acc)

    q = qkv_ref[0, mine, 0:HD]
    k = qkv_ref[0, seen, HD : 2 * HD]
    v = qkv_ref[0, seen, 2 * HD : 3 * HD]
    g = g_ref[0, mine, :]
    gap = (i * step - low).astype(jnp.int32)
    ahead = lax.broadcasted_iota(jnp.int32, (step, window), 1) - lax.broadcasted_iota(
        jnp.int32, (step, window), 0
    )
    allowed = (col_ref[mine, :] == row_ref[:, seen]) & (ahead <= gap)
    scores = jnp.where(allowed, dot_f32(q, k, NT) * scale, -1e30)
    top = jnp.max(scores, axis=1, keepdims=True)
    expos = jnp.where(allowed, jnp.exp(scores - top), 0.0)
    probs_f = expos * (1.0 / jnp.sum(expos, axis=1, keepdims=True))
    probs = probs_f.astype(jnp.bfloat16)
    att_ref[0, mine, :] = dot_f32(probs, v).astype(jnp.bfloat16)
    dprob = dot_f32(g, v, NT)
    delta = jnp.sum(probs_f * dprob, axis=1, keepdims=True)
    dscore = (probs_f * (dprob - delta)).astype(jnp.bfloat16)
    grad_ref[0, mine, 0:HD] = (dot_f32(dscore, k) * scale).astype(jnp.bfloat16)
    dk_acc[seen, :] += dot_f32(dscore, q, TN)
    dv_acc[seen, :] += dot_f32(probs, g, TN)

    @pl.when(i == pl.num_programs(1) - 1)
    def _():
        grad_ref[0, :, HD : 2 * HD] = (dk_acc[...] * scale).astype(jnp.bfloat16)
        grad_ref[0, :, 2 * HD : 3 * HD] = dv_acc[...].astype(jnp.bfloat16)


def attention(qkv, upstream, doc_ids, step):
    heads, rows, width = qkv.shape
    window = min((SPAN + 1) * step, rows)
    whole = lambda h, i: (h, 0, 0)
    fixed = lambda h, i: (0, 0)
    return pl.pallas_call(
        functools.partial(attention_kernel, step, window),
        out_shape=(
            jax.ShapeDtypeStruct((heads, rows, HD), jnp.bfloat16),
            jax.ShapeDtypeStruct((heads, rows, width), jnp.bfloat16),
        ),
        grid=(heads, rows // step),
        in_specs=[
            pl.BlockSpec((1, rows, width), whole),
            pl.BlockSpec((1, rows, HD), whole),
            pl.BlockSpec((rows, 1), fixed),
            pl.BlockSpec((1, rows), fixed),
        ],
        out_specs=[
            pl.BlockSpec((1, rows, HD), whole),
            pl.BlockSpec((1, rows, width), whole),
        ],
        scratch_shapes=[pltpu.VMEM((rows, HD), jnp.float32)] * 2,
        compiler_params=params(),
        name="attention",
    )(qkv, upstream, doc_ids[:, None], doc_ids[None, :])


def input_kernel(pair, mods_ref, d_ref, w_ref, out_ref, acc):
    step = pl.program_id(0)
    blocks = d_ref.shape[1] // BLOCK

    @pl.when(step == 0)
    def _():
        acc[...] = jnp.zeros_like(acc)

    def one(b, carry):
        rows = pl.ds(pl.multiple_of(b * BLOCK, BLOCK), BLOCK)
        modality = mods_ref[b]
        total = acc[rows, :]
        for p in range(3):
            lhs = jnp.concatenate(
                [d_ref[h, rows, p * HD : (p + 1) * HD] for h in range(pair)], axis=1
            )
            total = total + dot_f32(lhs, w_ref[modality, p], NT)
        acc[rows, :] = total
        return carry

    lax.fori_loop(0, blocks, one, 0, unroll=4)

    @pl.when(step == pl.num_programs(0) - 1)
    def _():
        out_ref[...] = acc[...].astype(jnp.bfloat16)


def input_parts(grads, planes, block_modality, pair):
    heads, rows, width3 = grads.shape
    width = planes.shape[2]
    return pl.pallas_call(
        functools.partial(input_kernel, pair),
        out_shape=jax.ShapeDtypeStruct((rows, width), jnp.bfloat16),
        grid_spec=pltpu.PrefetchScalarGridSpec(
            num_scalar_prefetch=1,
            grid=(heads // pair,),
            in_specs=[
                pl.BlockSpec((pair, rows, width3), lambda h, m: (h, 0, 0)),
                pl.BlockSpec((2, 3, width, pair * HD), lambda h, m: (0, 0, 0, h)),
            ],
            out_specs=pl.BlockSpec((rows, width), lambda h, m: (0, 0)),
            scratch_shapes=[pltpu.VMEM((rows, width), jnp.float32)],
        ),
        compiler_params=params(),
        name="input_parts",
    )(block_modality, grads, planes)


def weight_kernel(pair, d_ref, x_ref, out_ref):
    for p in range(3):
        rhs = jnp.concatenate([d_ref[h, :, p * HD : (p + 1) * HD] for h in range(pair)], axis=1)
        for modality in range(2):
            out_ref[modality, p] = dot_f32(x_ref[modality], rhs).astype(jnp.bfloat16)


def weight_grads(grads, flipped, pair):
    heads, rows, width3 = grads.shape
    width = flipped.shape[1]
    return pl.pallas_call(
        functools.partial(weight_kernel, pair),
        out_shape=jax.ShapeDtypeStruct((2, 3, width, heads * HD), jnp.bfloat16),
        grid=(heads // pair,),
        in_specs=[
            pl.BlockSpec((pair, rows, width3), lambda h: (h, 0, 0)),
            pl.BlockSpec((2, width, rows), lambda h: (0, 0, 0)),
        ],
        out_specs=pl.BlockSpec((2, 3, width, pair * HD), lambda h: (0, 0, 0, h)),
        compiler_params=params(),
        name="weight_grads",
    )(grads, flipped)


def place_inputs(parts):
    dp, mp = lax.axis_size("dp"), lax.axis_size("mp")
    ratio = dp // mp
    summed = lax.psum_scatter(parts, "mp", scatter_dimension=0, tiled=True)
    rows, width = summed.shape[0] // ratio, summed.shape[1]
    mine = lax.axis_index("dp")
    placed = jnp.zeros((rows, ratio * width), summed.dtype)
    for s in range(ratio):
        route = [
            (j * mp + g, (ratio * g + (j + s) % ratio) * mp + j // ratio)
            for j in range(dp)
            for g in range(mp)
        ]
        sent = lax.dynamic_slice_in_dim(summed, ((mine + s) % ratio) * rows, rows, 0)
        piece = lax.ppermute(sent, ("dp", "mp"), route)
        spot = (mine - s + ratio) % ratio
        placed = lax.dynamic_update_slice_in_dim(placed, piece, spot * width, 1)
    return placed


def by_heads(tokens, weights, block_modality, doc_ids, grad_out):
    local_rows = tokens.shape[0]
    head_width = weights.shape[3]
    heads = head_width // HD
    dp = lax.axis_size("dp")
    own = heads // dp
    total_rows = doc_ids.shape[0]
    pair = 2 if heads % 2 == 0 else 1
    columns = lax.all_to_all(tokens, "dp", split_axis=1, concat_axis=0, tiled=True)
    upstream = lax.all_to_all(
        grad_out.reshape(local_rows, heads, HD).transpose(1, 0, 2),
        "dp",
        split_axis=0,
        concat_axis=1,
        tiled=True,
    )
    planes = jnp.transpose(weights, (1, 2, 0, 3))
    partial = project(columns, planes, block_modality, pair)
    qkv = lax.psum_scatter(partial, "dp", scatter_dimension=0, tiled=True)
    attended, grads = attention(qkv, upstream, doc_ids, local_rows)
    attended = attended.reshape(own, dp, local_rows, HD).transpose(1, 0, 2, 3)
    attended = lax.all_to_all(attended, "dp", split_axis=0, concat_axis=0, tiled=True)
    attended = attended.reshape(heads, local_rows, HD)
    attended = attended.transpose(1, 0, 2).reshape(local_rows, head_width)
    gathered = lax.all_gather(grads, "dp", axis=0, tiled=True)
    token_mods = jnp.broadcast_to(block_modality[:, None], (total_rows // BLOCK, BLOCK))
    token_mods = token_mods.reshape(total_rows)
    mask = token_mods[None, :] == jnp.arange(2, dtype=jnp.int32)[:, None]
    flipped = jnp.where(mask[:, None, :], columns.T[None], jnp.zeros((), jnp.bfloat16))
    parts = input_parts(gathered, planes, block_modality, pair)
    grad_tokens = place_inputs(parts)
    grad_weights = jnp.transpose(weight_grads(gathered, flipped, pair), (2, 0, 1, 3))
    return attended, grad_tokens, grad_weights


def on_device(tokens, weights, block_modality, doc_ids, grad_out):
    dp, mp = lax.axis_size("dp"), lax.axis_size("mp")
    heads = weights.shape[3] // HD
    if heads % dp == 0 and dp % mp == 0:
        return by_heads(tokens, weights, block_modality, doc_ids, grad_out)
    return windowed(tokens, weights, block_modality, doc_ids, grad_out)


def solution(mesh):
    return jax.shard_map(
        on_device,
        mesh=mesh,
        in_specs=(P("dp", None), P("dp", None, None, "mp"), P(), P(), P("dp", "mp")),
        out_specs=(P("dp", "mp"), P("dp", "mp"), P("dp", None, None, "mp")),
        check_vma=False,
    )
```

```python
import functools

import jax
import jax.numpy as jnp
from jax import lax
from jax.experimental import pallas as pl
from jax.experimental.pallas import tpu as pltpu
from jax.sharding import PartitionSpec as P

HD = 128
BLOCK = 128
SPAN = 4


def shifted(block, axis, distance):
    devices = range(lax.axis_size(axis))
    route = [(i - distance, i) for i in devices if i - distance in devices]
    return lax.ppermute(block, axis, route)


def select_product(block_rows, modality, text_mat, image_mat, contract):
    contraction = (((1,), (contract,)), ((), ()))
    return lax.cond(
        modality == 0,
        lambda: lax.dot_general(
            block_rows, text_mat, contraction, preferred_element_type=jnp.float32
        ),
        lambda: lax.dot_general(
            block_rows, image_mat, contraction, preferred_element_type=jnp.float32
        ),
    )


def blockwise(row_data, modalities, text_mat, image_mat, contract):
    blocks = row_data.reshape(modalities.shape[0], BLOCK, row_data.shape[1])

    def one_block(block_pair):
        return select_product(block_pair[0], block_pair[1], text_mat, image_mat, contract)

    result = lax.map(one_block, (blocks, modalities))
    return result.reshape(row_data.shape[0], result.shape[2])


def windowed(tokens, weights, block_modality, doc_ids, grad_out):
    local_rows = tokens.shape[0]
    width_rows = weights.shape[0]
    head_width = weights.shape[3]
    head_count = head_width // HD
    dp_devices = lax.axis_size("dp")
    local_blocks = local_rows // BLOCK
    front_pad = SPAN * local_rows
    window_len = front_pad + local_rows
    my_index = lax.axis_index("dp")
    scale_factor = HD ** (-0.5)
    my_mods = lax.dynamic_slice_in_dim(block_modality, my_index * local_blocks, local_blocks, 0)
    flat_weights = weights.reshape(width_rows, 2, 3 * head_width)
    text_local = flat_weights[:, 0]
    image_local = flat_weights[:, 1]
    columns = lax.all_to_all(tokens, "dp", split_axis=1, concat_axis=0, tiled=True)
    text_whole, image_whole = (
        lax.all_gather(text_local, "dp", axis=0, tiled=True),
        lax.all_gather(image_local, "dp", axis=0, tiled=True),
    )
    summed = blockwise(tokens, my_mods, text_whole, image_whole, 0)
    qkv = summed.astype(jnp.bfloat16).reshape(local_rows, 3, head_count, HD)
    queries = qkv[:, 0]
    key_values = qkv[:, 1:]
    received = []
    for distance in range(SPAN, 0, -1):
        received.append(shifted(key_values, "dp", distance))
    window = jnp.concatenate(received + [key_values], 0)
    key_rows = window[:, 0]
    value_rows = window[:, 1]
    docs_pad = jnp.concatenate([jnp.full((front_pad,), -1, jnp.int32), doc_ids], 0)
    key_docs = lax.dynamic_slice_in_dim(docs_pad, my_index * local_rows, window_len, 0)
    query_docs = lax.dynamic_slice_in_dim(doc_ids, my_index * local_rows, local_rows, 0)
    offsets = jnp.arange(window_len, dtype=jnp.int32) - front_pad
    allowed = (key_docs[None, :] == query_docs[:, None]) & (
        offsets[None, :] <= jnp.arange(local_rows, dtype=jnp.int32)[:, None]
    )
    scores = (
        jnp.einsum("qhd,khd->hqk", queries, key_rows, preferred_element_type=jnp.float32)
        * scale_factor
    )
    scores = jnp.where(allowed[None], scores, -1e30)
    top_score = jnp.max(scores, axis=-1, keepdims=True)
    expos = jnp.where(allowed[None], jnp.exp(scores - top_score), 0.0)
    probs_f = expos / jnp.sum(expos, axis=-1, keepdims=True)
    probs = probs_f.astype(jnp.bfloat16)
    attended = jnp.einsum("hqk,khd->qhd", probs, value_rows, preferred_element_type=jnp.float32)
    attended = attended.astype(jnp.bfloat16).reshape(local_rows, head_width)
    upstream = grad_out.reshape(local_rows, head_count, HD)
    dprob = jnp.einsum("qhd,khd->hqk", upstream, value_rows, preferred_element_type=jnp.float32)
    row_delta = jnp.sum(probs_f * dprob, axis=-1, keepdims=True)
    dscore = (probs_f * (dprob - row_delta)).astype(jnp.bfloat16)
    grad_q = (
        jnp.einsum("hqk,khd->qhd", dscore, key_rows, preferred_element_type=jnp.float32)
        * scale_factor
    )
    grad_k = (
        jnp.einsum("hqk,qhd->khd", dscore, queries, preferred_element_type=jnp.float32)
        * scale_factor
    )
    grad_v = jnp.einsum("hqk,qhd->khd", probs, upstream, preferred_element_type=jnp.float32)
    window_grads = jnp.stack([grad_k, grad_v], 1)
    own_grads = window_grads[front_pad:]
    for distance in range(1, SPAN + 1):
        lower_edge = front_pad - distance * local_rows
        sent_block = window_grads[lower_edge : lower_edge + local_rows]
        own_grads = own_grads + shifted(sent_block.astype(jnp.bfloat16), "dp", -distance).astype(
            sent_block.dtype
        )
    dqkv = (
        jnp.concatenate([grad_q[:, None], own_grads], 1)
        .astype(jnp.bfloat16)
        .reshape(local_rows, 3 * head_width)
    )
    gathered = lax.all_gather(dqkv, "dp", axis=0, tiled=True)
    column_groups = columns.reshape(dp_devices, local_blocks, BLOCK, width_rows)
    grad_groups = gathered.reshape(dp_devices, local_blocks, BLOCK, 3 * head_width)
    modality_groups = block_modality.reshape(dp_devices, local_blocks)
    modality_range = jnp.arange(2, dtype=jnp.int32)

    def accumulate(running, triple):
        column_group, grad_group, group_mods = triple
        per_block = jnp.einsum(
            "bnf,bnc->bfc", column_group, grad_group, preferred_element_type=jnp.float32
        )
        selector = (group_mods[:, None] == modality_range[None, :]).astype(jnp.float32)
        return (running + jnp.sum(selector[:, :, None, None] * per_block[:, None], axis=0), None)

    weight_sum, unused = lax.scan(
        accumulate,
        jnp.zeros((2, width_rows, 3 * head_width), jnp.float32),
        (column_groups, grad_groups, modality_groups),
    )
    grad_weights = (
        jnp.transpose(weight_sum, (1, 0, 2))
        .astype(jnp.bfloat16)
        .reshape(width_rows, 2, 3, head_width)
    )
    input_terms = blockwise(dqkv, my_mods, text_whole, image_whole, 1)
    grad_tokens = lax.psum_scatter(
        input_terms.astype(jnp.bfloat16), "mp", scatter_dimension=1, tiled=True
    )
    return (attended, grad_tokens, grad_weights)


VMEM_LIMIT = 56 * 1024 * 1024
NT = (((1,), (1,)), ((), ()))
TN = (((0,), (0,)), ((), ()))


def dot_f32(a, b, dims=(((1,), (0,)), ((), ()))):
    return lax.dot_general(a, b, dims, preferred_element_type=jnp.float32)


def params():
    return pltpu.CompilerParams(vmem_limit_bytes=VMEM_LIMIT)


def cost(flops, moved):
    return pl.CostEstimate(flops=int(flops), bytes_accessed=int(moved), transcendentals=0)


def pair_blocks(mods):
    count = mods.shape[0]
    slots = jnp.arange(2 * (count // 2 + 1), dtype=jnp.int32)
    is_text = (mods == 0).astype(jnp.int32)
    texts = jnp.sum(is_text)
    index = jnp.arange(count, dtype=jnp.int32)
    before = (mods[None, :] == mods[:, None]) & (index[None, :] < index[:, None])
    rank = jnp.sum(before.astype(jnp.int32), axis=1)
    spot = jnp.where(mods == 0, rank, 2 * ((texts + 1) // 2) + rank)
    hit = spot[None, :] == slots[:, None]
    block = jnp.sum(jnp.where(hit, jnp.arange(count, dtype=jnp.int32)[None, :], 0), axis=1)
    pairs = block.reshape(-1, 2)
    full = jnp.any(hit, axis=1).reshape(-1, 2)
    second = jnp.where(full[:, 1], pairs[:, 1], pairs[:, 0])
    number = (texts + 1) // 2 + (count - texts + 1) // 2
    return jnp.stack([pairs[:, 0], second], 1).reshape(-1), number[None].astype(jnp.int32)


def block_rows(b):
    return pl.ds(pl.multiple_of(b * BLOCK, BLOCK), BLOCK)


def project_kernel(pair, mods_ref, order_ref, number_ref, x_ref, w_ref, out_ref):
    def one(n, carry):
        first, second = order_ref[2 * n], order_ref[2 * n + 1]
        x = jnp.concatenate([x_ref[block_rows(first), :], x_ref[block_rows(second), :]], axis=0)
        modality = mods_ref[first]
        for p in range(3):
            y = dot_f32(x, w_ref[modality, p]).astype(jnp.bfloat16)
            for h in range(pair):
                part = y[:, h * HD : (h + 1) * HD]
                out_ref[h, block_rows(first), p * HD : (p + 1) * HD] = part[:BLOCK]
                out_ref[h, block_rows(second), p * HD : (p + 1) * HD] = part[BLOCK:]
        return carry

    lax.fori_loop(0, number_ref[0], one, 0)


def project(columns, planes, block_modality, pair):
    rows, width = columns.shape
    heads = planes.shape[3] // HD
    order, number = pair_blocks(block_modality)
    return pl.pallas_call(
        functools.partial(project_kernel, pair),
        out_shape=jax.ShapeDtypeStruct((heads, rows, 3 * HD), jnp.bfloat16),
        grid_spec=pltpu.PrefetchScalarGridSpec(
            num_scalar_prefetch=3,
            grid=(heads // pair,),
            in_specs=[
                pl.BlockSpec((rows, width), lambda h, *_: (0, 0)),
                pl.BlockSpec((2, 3, width, pair * HD), lambda h, *_: (0, 0, 0, h)),
            ],
            out_specs=pl.BlockSpec((pair, rows, 3 * HD), lambda h, *_: (h, 0, 0)),
        ),
        compiler_params=params(),
        cost_estimate=cost(6 * rows * width * heads * HD, 6 * rows * heads * HD),
        name="project",
    )(block_modality, order, number, columns, planes)


def attention_kernel(step, window, chunks, qkv_ref, g_ref, col_ref, row_ref, att_ref, grad_ref, dk_acc, dv_acc):
    i = pl.program_id(1)
    scale = HD ** (-0.5)
    low = pl.multiple_of(jnp.maximum((i + 1) * step - window, 0), step)
    mine = pl.ds(pl.multiple_of(i * step, step), step)
    seen = pl.ds(low, window)

    @pl.when(i == 0)
    def _():
        dk_acc[...] = jnp.zeros_like(dk_acc)
        dv_acc[...] = jnp.zeros_like(dv_acc)

    q = qkv_ref[0, mine, 0:HD]
    k = qkv_ref[0, seen, HD : 2 * HD]
    v = qkv_ref[0, seen, 2 * HD : 3 * HD]
    g = g_ref[0, mine, :]
    gap = (i * step - low).astype(jnp.int32)
    ahead = lax.broadcasted_iota(jnp.int32, (step, window), 1) - lax.broadcasted_iota(
        jnp.int32, (step, window), 0
    )
    allowed = (col_ref[mine, :] == row_ref[:, seen]) & (ahead <= gap)
    scores = jnp.where(allowed, dot_f32(q, k, NT) * scale, -1e30)
    top = jnp.max(scores, axis=1, keepdims=True)
    expos = jnp.where(allowed, jnp.exp(scores - top), 0.0)
    probs_f = expos * (1.0 / jnp.sum(expos, axis=1, keepdims=True))
    probs = probs_f.astype(jnp.bfloat16)
    att_ref[0, mine, :] = dot_f32(probs, v).astype(jnp.bfloat16)
    dprob = dot_f32(g, v, NT)
    delta = jnp.sum(probs_f * dprob, axis=1, keepdims=True)
    dscore = (probs_f * (dprob - delta)).astype(jnp.bfloat16)
    place = pl.ds(pl.multiple_of((i // chunks) * step, step), step)
    grad_ref[0, lax.rem(i, chunks), place, 0:HD] = (dot_f32(dscore, k) * scale).astype(jnp.bfloat16)
    dk_acc[seen, :] += dot_f32(dscore, q, TN)
    dv_acc[seen, :] += dot_f32(probs, g, TN)

    @pl.when(i == pl.num_programs(1) - 1)
    def _():
        for block in range(dk_acc.shape[0] // step):
            rows = slice(block * step, (block + 1) * step)
            chunk, at = block % chunks, (block // chunks) * step
            spot = slice(at, at + step)
            grad_ref[0, chunk, spot, HD : 2 * HD] = (dk_acc[rows, :] * scale).astype(jnp.bfloat16)
            grad_ref[0, chunk, spot, 2 * HD : 3 * HD] = dv_acc[rows, :].astype(jnp.bfloat16)


def attention(qkv, upstream, doc_ids, step, chunks):
    heads, rows, width = qkv.shape
    window = min((SPAN + 1) * step, rows)
    whole = lambda h, i: (h, 0, 0)
    fixed = lambda h, i: (0, 0)
    return pl.pallas_call(
        functools.partial(attention_kernel, step, window, chunks),
        out_shape=(
            jax.ShapeDtypeStruct((heads, rows, HD), jnp.bfloat16),
            jax.ShapeDtypeStruct((heads, chunks, rows // chunks, width), jnp.bfloat16),
        ),
        grid=(heads, rows // step),
        in_specs=[
            pl.BlockSpec((1, rows, width), whole),
            pl.BlockSpec((1, rows, HD), whole),
            pl.BlockSpec((rows, 1), fixed),
            pl.BlockSpec((1, rows), fixed),
        ],
        out_specs=[
            pl.BlockSpec((1, rows, HD), whole),
            pl.BlockSpec((1, chunks, rows // chunks, width), lambda h, i: (h, 0, 0, 0)),
        ],
        cost_estimate=cost(10 * heads * rows * window * HD, 16 * heads * rows * HD),
        scratch_shapes=[pltpu.VMEM((rows, HD), jnp.float32)] * 2,
        compiler_params=params(),
        name="attention",
    )(qkv, upstream, doc_ids[:, None], doc_ids[None, :])


def input_kernel(pair, mods_ref, order_ref, number_ref, d_ref, w_ref, out_ref, acc):
    step = pl.program_id(0)

    @pl.when(step == 0)
    def _():
        acc[...] = jnp.zeros_like(acc)

    def one(n, carry):
        first, second = block_rows(order_ref[2 * n]), block_rows(order_ref[2 * n + 1])
        modality = mods_ref[order_ref[2 * n]]
        total = jnp.concatenate([acc[first, :], acc[second, :]], axis=0)
        for p in range(3):
            parts = [
                jnp.concatenate([d_ref[h, r, p * HD : (p + 1) * HD] for r in (first, second)], axis=0)
                for h in range(pair)
            ]
            total = total + dot_f32(jnp.concatenate(parts, axis=1), w_ref[modality, p], NT)
        acc[first, :] = total[:BLOCK]
        acc[second, :] = total[BLOCK:]
        return carry

    lax.fori_loop(0, number_ref[0], one, 0)

    @pl.when(step == pl.num_programs(0) - 1)
    def _():
        out_ref[...] = acc[...].astype(jnp.bfloat16)


def input_parts(grads, planes, mods, pair):
    heads, rows, width3 = grads.shape
    width = planes.shape[2]
    order, number = pair_blocks(mods)
    return pl.pallas_call(
        functools.partial(input_kernel, pair),
        out_shape=jax.ShapeDtypeStruct((rows, width), jnp.bfloat16),
        grid_spec=pltpu.PrefetchScalarGridSpec(
            num_scalar_prefetch=3,
            grid=(heads // pair,),
            in_specs=[
                pl.BlockSpec((pair, rows, width3), lambda h, *_: (h, 0, 0)),
                pl.BlockSpec((2, 3, width, pair * HD), lambda h, *_: (0, 0, 0, h)),
            ],
            out_specs=pl.BlockSpec((rows, width), lambda h, *_: (0, 0)),
            scratch_shapes=[pltpu.VMEM((rows, width), jnp.float32)],
        ),
        compiler_params=params(),
        cost_estimate=cost(6 * rows * width * heads * HD, 6 * rows * heads * HD),
        name="input_parts",
    )(mods, order, number, grads, planes)


def weight_kernel(pair, x_ref, *refs):
    d_refs, out_ref = refs[:-1], refs[-1]
    rows = d_refs[0].shape[1]
    for p in range(3):
        cols = slice(p * HD, (p + 1) * HD)
        rhs = [jnp.concatenate([d[h, :, cols] for h in range(pair)], axis=1) for d in d_refs]
        for modality in range(2):
            total = dot_f32(x_ref[modality, :, 0:rows], rhs[0])
            for c in range(1, len(rhs)):
                total = total + dot_f32(x_ref[modality, :, c * rows : (c + 1) * rows], rhs[c])
            out_ref[modality, p] = total.astype(jnp.bfloat16)


def weight_grads(gathered, flipped, pair):
    heads, rows, width3 = gathered[0].shape
    width, total_rows = flipped.shape[1:]
    return pl.pallas_call(
        functools.partial(weight_kernel, pair),
        out_shape=jax.ShapeDtypeStruct((2, 3, width, heads * HD), jnp.bfloat16),
        grid=(heads // pair,),
        in_specs=[pl.BlockSpec((2, width, total_rows), lambda h: (0, 0, 0))]
        + [pl.BlockSpec((pair, rows, width3), lambda h: (h, 0, 0))] * len(gathered),
        out_specs=pl.BlockSpec((2, 3, width, pair * HD), lambda h: (0, 0, 0, h)),
        compiler_params=params(),
        cost_estimate=cost(12 * total_rows * width * heads * HD, 6 * total_rows * heads * HD),
        name="weight_grads",
    )(flipped, *gathered)


def place_inputs(sums):
    dp, mp = lax.axis_size("dp"), lax.axis_size("mp")
    ratio = len(sums)
    rows, width = sums[0].shape
    mine = lax.axis_index("dp")
    placed = jnp.zeros((rows, ratio * width), sums[0].dtype)
    for s in range(ratio):
        route = [
            (j * mp + g, (ratio * g + (j + s) % ratio) * mp + j // ratio)
            for j in range(dp)
            for g in range(mp)
        ]
        chosen = (mine + s) % ratio
        sent = sums[0]
        for c in range(1, ratio):
            sent = jnp.where(chosen == c, sums[c], sent)
        piece = lax.ppermute(sent, ("dp", "mp"), route)
        spot = (mine - s + ratio) % ratio
        placed = lax.dynamic_update_slice_in_dim(placed, piece, spot * width, 1)
    return placed


def by_heads(tokens, weights, block_modality, doc_ids, grad_out):
    local_rows = tokens.shape[0]
    head_width = weights.shape[3]
    heads = head_width // HD
    dp = lax.axis_size("dp")
    own = heads // dp
    total_rows = doc_ids.shape[0]
    pair = 2 if heads % 2 == 0 else 1
    columns = lax.all_to_all(tokens, "dp", split_axis=1, concat_axis=0, tiled=True)
    upstream = lax.all_to_all(
        grad_out.reshape(local_rows, heads, HD).transpose(1, 0, 2),
        "dp",
        split_axis=0,
        concat_axis=1,
        tiled=True,
    )
    planes = jnp.transpose(weights, (1, 2, 0, 3))
    columns, upstream = lax.optimization_barrier((columns, upstream))
    mp = lax.axis_size("mp")
    chunks = dp // mp
    chunk_rows = total_rows // chunks
    dp_mods = block_modality.reshape(mp, chunks, local_rows // BLOCK)
    partial = project(columns, planes, block_modality, pair)
    qkv = lax.psum_scatter(
        partial.reshape(heads * total_rows, 3 * HD), "dp", scatter_dimension=0, tiled=True
    )
    token_mods = jnp.broadcast_to(
        dp_mods.transpose(1, 0, 2)[..., None], (chunks, mp, local_rows // BLOCK, BLOCK)
    ).reshape(total_rows)
    shuffled = columns.reshape(mp, chunks, local_rows, columns.shape[1]).transpose(1, 0, 2, 3)
    shuffled = shuffled.reshape(total_rows, columns.shape[1])
    mask = token_mods[None, :] == jnp.arange(2, dtype=jnp.int32)[:, None]
    flipped = jnp.where(mask[:, None, :], shuffled.T[None], jnp.zeros((), jnp.bfloat16))
    qkv, flipped = lax.optimization_barrier((qkv, flipped))
    qkv = qkv.reshape(own, total_rows, 3 * HD)
    attended, grads = attention(qkv, upstream, doc_ids, local_rows, chunks)
    gathered, sums = [], []
    for c in range(chunks):
        flat = grads[:, c].reshape(own * chunk_rows, 3 * HD)
        whole = lax.all_gather(flat, "dp", axis=0, tiled=True)
        gathered.append(whole.reshape(heads, chunk_rows, 3 * HD))
    for c in range(chunks):
        parts = input_parts(gathered[c], planes, dp_mods[:, c].reshape(-1), pair)
        sums.append(lax.psum_scatter(parts, "mp", scatter_dimension=0, tiled=True))
    attended = attended.reshape(own, dp, local_rows, HD).transpose(1, 0, 2, 3)
    attended = lax.all_to_all(attended, "dp", split_axis=0, concat_axis=0, tiled=True)
    attended = attended.reshape(heads, local_rows, HD)
    attended = attended.transpose(1, 0, 2).reshape(local_rows, head_width)
    by_plane = weight_grads(gathered, flipped, pair)
    by_plane, *sums = lax.optimization_barrier((by_plane, *sums))
    grad_tokens = place_inputs(sums)
    grad_weights = jnp.transpose(by_plane, (2, 0, 1, 3))
    return attended, grad_tokens, grad_weights


def on_device(tokens, weights, block_modality, doc_ids, grad_out):
    dp, mp = lax.axis_size("dp"), lax.axis_size("mp")
    heads = weights.shape[3] // HD
    if heads % dp == 0 and dp % mp == 0:
        return by_heads(tokens, weights, block_modality, doc_ids, grad_out)
    return windowed(tokens, weights, block_modality, doc_ids, grad_out)


def solution(mesh):
    return jax.shard_map(
        on_device,
        mesh=mesh,
        in_specs=(P("dp", None), P("dp", None, None, "mp"), P(), P(), P("dp", "mp")),
        out_specs=(P("dp", "mp"), P("dp", "mp"), P("dp", None, None, "mp")),
        check_vma=False,
    )
```

```python
import functools

import jax
import jax.numpy as jnp
from jax import lax
from jax.experimental import pallas as pl
from jax.experimental.pallas import tpu as pltpu
from jax.sharding import PartitionSpec as P

HD = 128
BLOCK = 128
SPAN = 4


def shifted(block, axis, distance):
    devices = range(lax.axis_size(axis))
    route = [(i - distance, i) for i in devices if i - distance in devices]
    return lax.ppermute(block, axis, route)


def select_product(block_rows, modality, text_mat, image_mat, contract):
    contraction = (((1,), (contract,)), ((), ()))
    return lax.cond(
        modality == 0,
        lambda: lax.dot_general(
            block_rows, text_mat, contraction, preferred_element_type=jnp.float32
        ),
        lambda: lax.dot_general(
            block_rows, image_mat, contraction, preferred_element_type=jnp.float32
        ),
    )


def blockwise(row_data, modalities, text_mat, image_mat, contract):
    blocks = row_data.reshape(modalities.shape[0], BLOCK, row_data.shape[1])

    def one_block(block_pair):
        return select_product(block_pair[0], block_pair[1], text_mat, image_mat, contract)

    result = lax.map(one_block, (blocks, modalities))
    return result.reshape(row_data.shape[0], result.shape[2])


def windowed(tokens, weights, block_modality, doc_ids, grad_out):
    local_rows = tokens.shape[0]
    width_rows = weights.shape[0]
    head_width = weights.shape[3]
    head_count = head_width // HD
    dp_devices = lax.axis_size("dp")
    local_blocks = local_rows // BLOCK
    front_pad = SPAN * local_rows
    window_len = front_pad + local_rows
    my_index = lax.axis_index("dp")
    scale_factor = HD ** (-0.5)
    my_mods = lax.dynamic_slice_in_dim(block_modality, my_index * local_blocks, local_blocks, 0)
    flat_weights = weights.reshape(width_rows, 2, 3 * head_width)
    text_local = flat_weights[:, 0]
    image_local = flat_weights[:, 1]
    columns = lax.all_to_all(tokens, "dp", split_axis=1, concat_axis=0, tiled=True)
    text_whole, image_whole = (
        lax.all_gather(text_local, "dp", axis=0, tiled=True),
        lax.all_gather(image_local, "dp", axis=0, tiled=True),
    )
    summed = blockwise(tokens, my_mods, text_whole, image_whole, 0)
    qkv = summed.astype(jnp.bfloat16).reshape(local_rows, 3, head_count, HD)
    queries = qkv[:, 0]
    key_values = qkv[:, 1:]
    received = []
    for distance in range(SPAN, 0, -1):
        received.append(shifted(key_values, "dp", distance))
    window = jnp.concatenate(received + [key_values], 0)
    key_rows = window[:, 0]
    value_rows = window[:, 1]
    docs_pad = jnp.concatenate([jnp.full((front_pad,), -1, jnp.int32), doc_ids], 0)
    key_docs = lax.dynamic_slice_in_dim(docs_pad, my_index * local_rows, window_len, 0)
    query_docs = lax.dynamic_slice_in_dim(doc_ids, my_index * local_rows, local_rows, 0)
    offsets = jnp.arange(window_len, dtype=jnp.int32) - front_pad
    allowed = (key_docs[None, :] == query_docs[:, None]) & (
        offsets[None, :] <= jnp.arange(local_rows, dtype=jnp.int32)[:, None]
    )
    scores = (
        jnp.einsum("qhd,khd->hqk", queries, key_rows, preferred_element_type=jnp.float32)
        * scale_factor
    )
    scores = jnp.where(allowed[None], scores, -1e30)
    top_score = jnp.max(scores, axis=-1, keepdims=True)
    expos = jnp.where(allowed[None], jnp.exp(scores - top_score), 0.0)
    probs_f = expos / jnp.sum(expos, axis=-1, keepdims=True)
    probs = probs_f.astype(jnp.bfloat16)
    attended = jnp.einsum("hqk,khd->qhd", probs, value_rows, preferred_element_type=jnp.float32)
    attended = attended.astype(jnp.bfloat16).reshape(local_rows, head_width)
    upstream = grad_out.reshape(local_rows, head_count, HD)
    dprob = jnp.einsum("qhd,khd->hqk", upstream, value_rows, preferred_element_type=jnp.float32)
    row_delta = jnp.sum(probs_f * dprob, axis=-1, keepdims=True)
    dscore = (probs_f * (dprob - row_delta)).astype(jnp.bfloat16)
    grad_q = (
        jnp.einsum("hqk,khd->qhd", dscore, key_rows, preferred_element_type=jnp.float32)
        * scale_factor
    )
    grad_k = (
        jnp.einsum("hqk,qhd->khd", dscore, queries, preferred_element_type=jnp.float32)
        * scale_factor
    )
    grad_v = jnp.einsum("hqk,qhd->khd", probs, upstream, preferred_element_type=jnp.float32)
    window_grads = jnp.stack([grad_k, grad_v], 1)
    own_grads = window_grads[front_pad:]
    for distance in range(1, SPAN + 1):
        lower_edge = front_pad - distance * local_rows
        sent_block = window_grads[lower_edge : lower_edge + local_rows]
        own_grads = own_grads + shifted(sent_block.astype(jnp.bfloat16), "dp", -distance).astype(
            sent_block.dtype
        )
    dqkv = (
        jnp.concatenate([grad_q[:, None], own_grads], 1)
        .astype(jnp.bfloat16)
        .reshape(local_rows, 3 * head_width)
    )
    gathered = lax.all_gather(dqkv, "dp", axis=0, tiled=True)
    column_groups = columns.reshape(dp_devices, local_blocks, BLOCK, width_rows)
    grad_groups = gathered.reshape(dp_devices, local_blocks, BLOCK, 3 * head_width)
    modality_groups = block_modality.reshape(dp_devices, local_blocks)
    modality_range = jnp.arange(2, dtype=jnp.int32)

    def accumulate(running, triple):
        column_group, grad_group, group_mods = triple
        per_block = jnp.einsum(
            "bnf,bnc->bfc", column_group, grad_group, preferred_element_type=jnp.float32
        )
        selector = (group_mods[:, None] == modality_range[None, :]).astype(jnp.float32)
        return (running + jnp.sum(selector[:, :, None, None] * per_block[:, None], axis=0), None)

    weight_sum, unused = lax.scan(
        accumulate,
        jnp.zeros((2, width_rows, 3 * head_width), jnp.float32),
        (column_groups, grad_groups, modality_groups),
    )
    grad_weights = (
        jnp.transpose(weight_sum, (1, 0, 2))
        .astype(jnp.bfloat16)
        .reshape(width_rows, 2, 3, head_width)
    )
    input_terms = blockwise(dqkv, my_mods, text_whole, image_whole, 1)
    grad_tokens = lax.psum_scatter(
        input_terms.astype(jnp.bfloat16), "mp", scatter_dimension=1, tiled=True
    )
    return (attended, grad_tokens, grad_weights)


VMEM_LIMIT = 56 * 1024 * 1024
NT = (((1,), (1,)), ((), ()))
TN = (((0,), (0,)), ((), ()))


def dot_f32(a, b, dims=(((1,), (0,)), ((), ()))):
    return lax.dot_general(a, b, dims, preferred_element_type=jnp.float32)


def params():
    return pltpu.CompilerParams(vmem_limit_bytes=VMEM_LIMIT)


def cost(flops, moved):
    return pl.CostEstimate(flops=int(flops), bytes_accessed=int(moved), transcendentals=0)


def pair_blocks(mods):
    count = mods.shape[0]
    slots = jnp.arange(2 * (count // 2 + 1), dtype=jnp.int32)
    is_text = (mods == 0).astype(jnp.int32)
    texts = jnp.sum(is_text)
    index = jnp.arange(count, dtype=jnp.int32)
    before = (mods[None, :] == mods[:, None]) & (index[None, :] < index[:, None])
    rank = jnp.sum(before.astype(jnp.int32), axis=1)
    spot = jnp.where(mods == 0, rank, 2 * ((texts + 1) // 2) + rank)
    hit = spot[None, :] == slots[:, None]
    block = jnp.sum(jnp.where(hit, jnp.arange(count, dtype=jnp.int32)[None, :], 0), axis=1)
    pairs = block.reshape(-1, 2)
    full = jnp.any(hit, axis=1).reshape(-1, 2)
    second = jnp.where(full[:, 1], pairs[:, 1], pairs[:, 0])
    number = (texts + 1) // 2 + (count - texts + 1) // 2
    return jnp.stack([pairs[:, 0], second], 1).reshape(-1), number[None].astype(jnp.int32)


def block_rows(b):
    return pl.ds(pl.multiple_of(b * BLOCK, BLOCK), BLOCK)


def columns_of(i, p):
    return pl.ds(pl.multiple_of(i * (3 * HD) + p * HD, HD), HD)


def spot_of(b, step, p):
    per = step // BLOCK
    return block_rows(lax.rem(b, per)), columns_of(b // per, p)


def project_kernel(step, pair, mods_ref, order_ref, number_ref, x_ref, w_ref, out_ref):
    def one(n, carry):
        first, second = order_ref[2 * n], order_ref[2 * n + 1]
        x = jnp.concatenate([x_ref[block_rows(first), :], x_ref[block_rows(second), :]], axis=0)
        modality = mods_ref[first]
        for p in range(3):
            y = dot_f32(x, w_ref[modality, p]).astype(jnp.bfloat16)
            for h in range(pair):
                part = y[:, h * HD : (h + 1) * HD]
                out_ref[(h, *spot_of(first, step, p))] = part[:BLOCK]
                out_ref[(h, *spot_of(second, step, p))] = part[BLOCK:]
        return carry

    lax.fori_loop(0, number_ref[0], one, 0)


def project(columns, planes, block_modality, pair, step):
    rows, width = columns.shape
    heads = planes.shape[3] // HD
    order, number = pair_blocks(block_modality)
    return pl.pallas_call(
        functools.partial(project_kernel, step, pair),
        out_shape=jax.ShapeDtypeStruct((heads, step, rows // step * 3 * HD), jnp.bfloat16),
        grid_spec=pltpu.PrefetchScalarGridSpec(
            num_scalar_prefetch=3,
            grid=(heads // pair,),
            in_specs=[
                pl.BlockSpec((rows, width), lambda h, *_: (0, 0)),
                pl.BlockSpec((2, 3, width, pair * HD), lambda h, *_: (0, 0, 0, h)),
            ],
            out_specs=pl.BlockSpec((pair, step, rows // step * 3 * HD), lambda h, *_: (h, 0, 0)),
        ),
        compiler_params=params(),
        cost_estimate=cost(6 * rows * width * heads * HD, 6 * rows * heads * HD),
        name="project",
    )(block_modality, order, number, columns, planes)


def attention_kernel(step, window, qkv_ref, g_ref, col_ref, row_ref, att_ref, grad_ref, dk_acc, dv_acc):
    i = pl.program_id(1)
    scale = HD ** (-0.5)
    low = pl.multiple_of(jnp.maximum((i + 1) * step - window, 0), step)
    mine = pl.ds(pl.multiple_of(i * step, step), step)
    seen = pl.ds(low, window)

    @pl.when(i == 0)
    def _():
        dk_acc[...] = jnp.zeros_like(dk_acc)
        dv_acc[...] = jnp.zeros_like(dv_acc)

    first = low // step
    spread = range(window // step)
    q = qkv_ref[0, :, columns_of(i, 0)]
    k = jnp.concatenate([qkv_ref[0, :, columns_of(first + j, 1)] for j in spread], axis=0)
    v = jnp.concatenate([qkv_ref[0, :, columns_of(first + j, 2)] for j in spread], axis=0)
    g = g_ref[0, mine, :]
    gap = (i * step - low).astype(jnp.int32)
    ahead = lax.broadcasted_iota(jnp.int32, (step, window), 1) - lax.broadcasted_iota(
        jnp.int32, (step, window), 0
    )
    allowed = (col_ref[mine, :] == row_ref[:, seen]) & (ahead <= gap)
    scores = jnp.where(allowed, dot_f32(q, k, NT) * scale, -1e30)
    top = jnp.max(scores, axis=1, keepdims=True)
    expos = jnp.where(allowed, jnp.exp(scores - top), 0.0)
    probs_f = expos * (1.0 / jnp.sum(expos, axis=1, keepdims=True))
    probs = probs_f.astype(jnp.bfloat16)
    att_ref[0, mine, :] = dot_f32(probs, v).astype(jnp.bfloat16)
    dprob = dot_f32(g, v, NT)
    delta = jnp.sum(probs_f * dprob, axis=1, keepdims=True)
    dscore = (probs_f * (dprob - delta)).astype(jnp.bfloat16)
    grad_ref[0, :, columns_of(i, 0)] = (dot_f32(dscore, k) * scale).astype(jnp.bfloat16)
    dk_acc[seen, :] += dot_f32(dscore, q, TN)
    dv_acc[seen, :] += dot_f32(probs, g, TN)

    @pl.when(i == pl.num_programs(1) - 1)
    def _():
        for block in range(dk_acc.shape[0] // step):
            rows = slice(block * step, (block + 1) * step)
            at = (3 * block + 1) * HD
            grad_ref[0, :, at : at + HD] = (dk_acc[rows, :] * scale).astype(jnp.bfloat16)
            grad_ref[0, :, at + HD : at + 2 * HD] = dv_acc[rows, :].astype(jnp.bfloat16)


def attention(qkv, upstream, doc_ids, step):
    heads, rows = upstream.shape[:2]
    window = min((SPAN + 1) * step, rows)
    whole = lambda h, i: (h, 0, 0)
    fixed = lambda h, i: (0, 0)
    return pl.pallas_call(
        functools.partial(attention_kernel, step, window),
        out_shape=(
            jax.ShapeDtypeStruct((heads, rows, HD), jnp.bfloat16),
            jax.ShapeDtypeStruct(qkv.shape, jnp.bfloat16),
        ),
        grid=(heads, rows // step),
        in_specs=[
            pl.BlockSpec((1,) + qkv.shape[1:], whole),
            pl.BlockSpec((1, rows, HD), whole),
            pl.BlockSpec((rows, 1), fixed),
            pl.BlockSpec((1, rows), fixed),
        ],
        out_specs=[
            pl.BlockSpec((1, rows, HD), whole),
            pl.BlockSpec((1,) + qkv.shape[1:], whole),
        ],
        cost_estimate=cost(10 * heads * rows * window * HD, 16 * heads * rows * HD),
        scratch_shapes=[pltpu.VMEM((rows, HD), jnp.float32)] * 2,
        compiler_params=params(),
        name="attention",
    )(qkv, upstream, doc_ids[:, None], doc_ids[None, :])


def input_kernel(pair, mods_ref, order_ref, number_ref, d_ref, w_ref, out_ref, acc):
    step = pl.program_id(0)
    step_rows = d_ref.shape[1]

    @pl.when(step == 0)
    def _():
        acc[...] = jnp.zeros_like(acc)

    def one(n, carry):
        both = (order_ref[2 * n], order_ref[2 * n + 1])
        first, second = block_rows(both[0]), block_rows(both[1])
        modality = mods_ref[order_ref[2 * n]]
        total = jnp.concatenate([acc[first, :], acc[second, :]], axis=0)
        for p in range(3):
            parts = [
                jnp.concatenate([d_ref[(h, *spot_of(b, step_rows, p))] for b in both], axis=0)
                for h in range(pair)
            ]
            total = total + dot_f32(jnp.concatenate(parts, axis=1), w_ref[modality, p], NT)
        acc[first, :] = total[:BLOCK]
        acc[second, :] = total[BLOCK:]
        return carry

    lax.fori_loop(0, number_ref[0], one, 0)

    @pl.when(step == pl.num_programs(0) - 1)
    def _():
        out_ref[...] = acc[...].astype(jnp.bfloat16)


def input_parts(grads, planes, mods, pair):
    heads, step, spread = grads.shape
    rows = step * spread // (3 * HD)
    width = planes.shape[2]
    order, number = pair_blocks(mods)
    return pl.pallas_call(
        functools.partial(input_kernel, pair),
        out_shape=jax.ShapeDtypeStruct((rows, width), jnp.bfloat16),
        grid_spec=pltpu.PrefetchScalarGridSpec(
            num_scalar_prefetch=3,
            grid=(heads // pair,),
            in_specs=[
                pl.BlockSpec((pair, step, spread), lambda h, *_: (h, 0, 0)),
                pl.BlockSpec((2, 3, width, pair * HD), lambda h, *_: (0, 0, 0, h)),
            ],
            out_specs=pl.BlockSpec((rows, width), lambda h, *_: (0, 0)),
            scratch_shapes=[pltpu.VMEM((rows, width), jnp.float32)],
        ),
        compiler_params=params(),
        cost_estimate=cost(6 * rows * width * heads * HD, 6 * rows * heads * HD),
        name="input_parts",
    )(mods, order, number, grads, planes)


def weight_kernel(pair, x_ref, d_ref, out_ref):
    for p in range(3):
        starts = range(p * HD, d_ref.shape[2], 3 * HD)
        rhs = jnp.concatenate(
            [
                jnp.concatenate([d_ref[h, :, at : at + HD] for h in range(pair)], axis=1)
                for at in starts
            ],
            axis=0,
        )
        for modality in range(2):
            out_ref[modality, p] = dot_f32(x_ref[modality], rhs).astype(jnp.bfloat16)


def weight_grads(gathered, flipped, pair):
    heads, step, spread = gathered.shape
    width, total_rows = flipped.shape[1:]
    return pl.pallas_call(
        functools.partial(weight_kernel, pair),
        out_shape=jax.ShapeDtypeStruct((2, 3, width, heads * HD), jnp.bfloat16),
        grid=(heads // pair,),
        in_specs=[
            pl.BlockSpec((2, width, total_rows), lambda h: (0, 0, 0)),
            pl.BlockSpec((pair, step, spread), lambda h: (h, 0, 0)),
        ],
        out_specs=pl.BlockSpec((2, 3, width, pair * HD), lambda h: (0, 0, 0, h)),
        compiler_params=params(),
        cost_estimate=cost(12 * total_rows * width * heads * HD, 6 * total_rows * heads * HD),
        name="weight_grads",
    )(flipped, gathered)


def place_inputs(sums):
    dp, mp = lax.axis_size("dp"), lax.axis_size("mp")
    ratio = len(sums)
    rows, width = sums[0].shape
    mine = lax.axis_index("dp")
    placed = jnp.zeros((rows, ratio * width), sums[0].dtype)
    for s in range(ratio):
        route = [
            (j * mp + g, (ratio * g + (j + s) % ratio) * mp + j // ratio)
            for j in range(dp)
            for g in range(mp)
        ]
        chosen = (mine + s) % ratio
        sent = sums[0]
        for c in range(1, ratio):
            sent = jnp.where(chosen == c, sums[c], sent)
        piece = lax.ppermute(sent, ("dp", "mp"), route)
        spot = (mine - s + ratio) % ratio
        placed = lax.dynamic_update_slice_in_dim(placed, piece, spot * width, 1)
    return placed


def by_heads(tokens, weights, block_modality, doc_ids, grad_out):
    local_rows = tokens.shape[0]
    head_width = weights.shape[3]
    heads = head_width // HD
    dp = lax.axis_size("dp")
    own = heads // dp
    total_rows = doc_ids.shape[0]
    pair = 2 if heads % 2 == 0 else 1
    columns = lax.all_to_all(tokens, "dp", split_axis=1, concat_axis=0, tiled=True)
    upstream = lax.all_to_all(
        grad_out.reshape(local_rows, heads, HD).transpose(1, 0, 2),
        "dp",
        split_axis=0,
        concat_axis=1,
        tiled=True,
    )
    planes = jnp.transpose(weights, (1, 2, 0, 3))
    mp = lax.axis_size("mp")
    chunks = dp // mp
    partial = project(columns, planes, block_modality, pair, local_rows)
    spread = dp * 3 * HD
    qkv = lax.psum_scatter(
        partial.reshape(heads * local_rows, spread), "dp", scatter_dimension=0, tiled=True
    )
    token_mods = jnp.broadcast_to(block_modality[:, None], (total_rows // BLOCK, BLOCK))
    mask = token_mods.reshape(1, total_rows) == jnp.arange(2, dtype=jnp.int32)[:, None]
    flipped = jnp.where(mask[:, None, :], columns.T[None], jnp.zeros((), jnp.bfloat16))
    qkv, flipped = lax.optimization_barrier((qkv, flipped))
    qkv = qkv.reshape(own, local_rows, spread)
    attended, grads = attention(qkv, upstream, doc_ids, local_rows)
    grads = lax.optimization_barrier(grads.reshape(own * local_rows, spread))
    gathered = lax.optimization_barrier(lax.all_gather(grads, "dp", axis=0, tiled=True))
    gathered = gathered.reshape(heads, local_rows, spread)
    parts = input_parts(gathered, planes, block_modality, pair)
    summed = lax.psum_scatter(parts, "mp", scatter_dimension=0, tiled=True)
    attended = attended.reshape(own, dp, local_rows, HD).transpose(1, 0, 2, 3)
    attended = lax.all_to_all(attended, "dp", split_axis=0, concat_axis=0, tiled=True)
    attended = attended.reshape(heads, local_rows, HD)
    attended = attended.transpose(1, 0, 2).reshape(local_rows, head_width)
    by_plane = weight_grads(gathered, flipped, pair)
    by_plane, summed = lax.optimization_barrier((by_plane, summed))
    grad_tokens = place_inputs(jnp.split(summed, chunks, axis=0))
    grad_weights = jnp.transpose(by_plane, (2, 0, 1, 3))
    return attended, grad_tokens, grad_weights


def on_device(tokens, weights, block_modality, doc_ids, grad_out):
    dp, mp = lax.axis_size("dp"), lax.axis_size("mp")
    heads = weights.shape[3] // HD
    if heads % dp == 0 and dp % mp == 0:
        return by_heads(tokens, weights, block_modality, doc_ids, grad_out)
    return windowed(tokens, weights, block_modality, doc_ids, grad_out)


def solution(mesh):
    return jax.shard_map(
        on_device,
        mesh=mesh,
        in_specs=(P("dp", None), P("dp", None, None, "mp"), P(), P(), P("dp", "mp")),
        out_specs=(P("dp", "mp"), P("dp", "mp"), P("dp", None, None, "mp")),
        check_vma=False,
    )
```
